256 devices in a mesh: seq: 32 (over z_lo, x, core), vocab: 8 (over z_hi, y).
Axes of the slice: x: 4, y: 4, z: 8 (z_hi: 2, z_lo: 4; z = z_hi * 4 + z_lo), core: 2. Of those that a mesh axis runs over, the one named last changes fastest.
Arguments:
- queries: bfloat16 [3, 8192, 8192], P(None, 'seq', 'vocab'), may hold values from -32 to 32
- draft_kv: bfloat16 [3, 2, 8192, 1024], P(None, None, 'seq', 'vocab'), may hold values from -6 to 6
- doc_ids: int32 [8192], P('seq'), may hold values from 0 to 8, as said below
- logits: bfloat16 [8192, 65536], P('seq', 'vocab'), may hold values from -90 to 360
- targets: int32 [8192], P('seq'), may hold values from 0 to 65535
Outputs:
- attended: bfloat16 [3, 8192, 8192], P(None, 'seq', 'vocab')
- row_peak: float32 [3, 8192, 64], P(None, 'seq', 'vocab')
- token_loss: float32 [8192], P('seq')
The draws below stay inside these ranges and needn't reach their ends.
Inputs may be any that keep to these rules, and one draw needn't show every extreme that they name: `doc_ids`: document ids start at 0, never fall, and rise by one where a new document begins; one document has exactly 6144 tokens, and the other tokens form exactly (8192 - 6144) // 256 documents, each shorter than it.
All inputs are finite; a program needn't handle non-finite values.
Results may differ from the reference program's by a relative error of at most 0.004.
Values may be sent and summed in bfloat16 or wider, within the bound.
A program may use at most 64 MiB of HBM per device.

```python
import math
import jax
import jax.numpy as jnp
from jax import lax

HEADS = 64
KV = 8
HD = 128
VOCAB = 65536
STEPS = 3
TOK_DEV = 256
TOKENS = 8192
LONG_DOC = 6144


def doc_layout(key):
    base_key = jax.random.fold_in(key, 101)
    cut_key, pick_key = jax.random.split(base_key)
    outside = TOKENS - LONG_DOC
    pieces = outside // TOK_DEV
    shuffled = jax.random.permutation(cut_key, outside - 1) + 1
    cuts = shuffled[:pieces - 1]
    bounds = jnp.sort(jnp.concatenate([jnp.zeros((1,), jnp.int32), cuts.astype(jnp.int32), jnp.full((1,), outside, jnp.int32)]))
    offset = bounds[jax.random.randint(pick_key, (), 0, pieces + 1)]
    position = jnp.arange(TOKENS, dtype=jnp.int32)
    inside = (position >= offset) & (position < offset + LONG_DOC)
    outer = jnp.where(position >= offset + LONG_DOC, position - LONG_DOC, position)
    is_cut = (outer == 0) | jnp.any(outer[:, None] == cuts[None, :].astype(jnp.int32), axis=1)
    begins = jnp.where(inside, position == offset, is_cut)
    running = jnp.cumsum(begins.astype(jnp.int32))
    return (running - 1).astype(jnp.int32)


def draw_doc_ids(key, part):
    return doc_layout(key)


def draw_draft_kv(key, part):
    draw_key = jax.random.fold_in(key, 303)
    shape_all = (STEPS, 2, TOKENS, KV, HD)
    values = jnp.clip(jax.random.normal(draw_key, shape_all, jnp.float32), -6.0, 6.0)
    return values.reshape(STEPS, 2, TOKENS, KV * HD).astype(jnp.bfloat16)


def draw_queries(key, part):
    draw_key = jax.random.fold_in(key, 404)
    group_size = HEADS // KV
    shape_all = (STEPS, TOKENS, KV, group_size, HD)
    values = jnp.clip(jax.random.normal(draw_key, shape_all, jnp.float32), -6.0, 6.0)
    return values.reshape(STEPS, TOKENS, HEADS * HD).astype(jnp.bfloat16)


def draw_logits(key, part):
    draw_key = jax.random.fold_in(key, 505)
    normal_key = jax.random.fold_in(draw_key, 0)
    noise = jax.random.normal(normal_key, (TOKENS, VOCAB), jnp.float32)
    values = jnp.clip(3.0 * noise, -18.0, 18.0)
    return values.astype(jnp.bfloat16)


def plant(entries, key, low, high):
    longest = entries.shape.index(max(entries.shape))
    spots = []
    for shift in (0, 1):
        where = [jax.random.randint(jax.random.fold_in(key, axis), (), 0, length) for axis, length in enumerate(entries.shape)]
        where[longest] = (where[longest] + shift) % entries.shape[longest]
        spots.append(tuple(where))
    return entries.at[spots[0]].set(low).at[spots[1]].set(high)


def setup_inputs(seed: int = 0) -> dict:
    arg_keys = jax.random.split(jax.random.key(seed), 6)
    return {
        "queries": draw_queries(jax.random.fold_in(arg_keys[5], 71), 0),
        "draft_kv": draw_draft_kv(jax.random.fold_in(arg_keys[5], 71), 0),
        "doc_ids": draw_doc_ids(jax.random.fold_in(arg_keys[5], 71), 0),
        "logits": draw_logits(jax.random.fold_in(arg_keys[5], 71), 0),
        "targets": plant(jax.random.randint(arg_keys[4], (TOKENS,), 0, VOCAB), jax.random.fold_in(arg_keys[4], 1), 0, VOCAB - 1).astype(jnp.int32),
    }


negative_fill = -1e30


def attend_step(step_index, queries, draft_kv, doc_ids):
    group_size = HEADS // KV
    block_width = math.gcd(TOKENS, 512)
    score_scale = HD ** -0.5
    query_all = queries[step_index].reshape(TOKENS, KV, group_size, HD)
    key_all = draft_kv[0, 0].reshape(TOKENS, KV, HD)
    value_all = draft_kv[0, 1].reshape(TOKENS, KV, HD)
    diagonal_pairs = [(draft_kv[earlier, 0].reshape(TOKENS, KV, HD), draft_kv[earlier, 1].reshape(TOKENS, KV, HD)) for earlier in range(1, step_index + 1)]

    def one_block(block_index):
        block_start = block_index * block_width
        query_rows = lax.dynamic_slice_in_dim(query_all, block_start, block_width, 0).astype(jnp.float32)
        query_pos = block_start + jnp.arange(block_width, dtype=jnp.int32)
        query_docs = lax.dynamic_slice_in_dim(doc_ids, block_start, block_width, 0)

        def scores_at(key_index):
            key_start = key_index * block_width
            key_rows = lax.dynamic_slice_in_dim(key_all, key_start, block_width, 0).astype(jnp.float32)
            scores = jnp.einsum("tkgd,skd->tkgs", query_rows, key_rows) * score_scale
            key_pos = key_start + jnp.arange(block_width, dtype=jnp.int32)
            key_docs = lax.dynamic_slice_in_dim(doc_ids, key_start, block_width, 0)
            usable = (key_pos[None, :] <= query_pos[:, None]) & (key_docs[None, :] == query_docs[:, None])
            return scores, usable[:, None, None, :], key_start

        def take_max(key_index, highest):
            scores, usable, key_start = scores_at(key_index)
            return jnp.maximum(highest, jnp.max(jnp.where(usable, scores, negative_fill), axis=3))

        row_peak = lax.fori_loop(0, block_index + 1, take_max, jnp.full((block_width, KV, group_size), negative_fill, jnp.float32))
        diagonal_scores = []
        for diag_keys, diag_values in diagonal_pairs:
            diag_rows = lax.dynamic_slice_in_dim(diag_keys, block_start, block_width, 0).astype(jnp.float32)
            diag_score = jnp.einsum("tkgd,tkd->tkg", query_rows, diag_rows) * score_scale
            diagonal_scores.append(diag_score)
            row_peak = jnp.maximum(row_peak, diag_score)

        def add_terms(key_index, state):
            denominator, accumulated = state
            scores, usable, key_start = scores_at(key_index)
            weights = jnp.where(usable, jnp.exp(scores - row_peak[..., None]), 0.0)
            rounded = lax.optimization_barrier(weights.astype(jnp.bfloat16)).astype(jnp.float32)
            value_rows = lax.dynamic_slice_in_dim(value_all, key_start, block_width, 0).astype(jnp.float32)
            accumulated = accumulated + jnp.einsum("tkgs,skd->tkgd", rounded, value_rows)
            return denominator + jnp.sum(weights, axis=3), accumulated

        start_state = (jnp.zeros((block_width, KV, group_size), jnp.float32), jnp.zeros((block_width, KV, group_size, HD), jnp.float32))
        denominator, accumulated = lax.fori_loop(0, block_index + 1, add_terms, start_state)
        for diag_score, pair in zip(diagonal_scores, diagonal_pairs):
            diag_weight = jnp.exp(diag_score - row_peak)
            denominator = denominator + diag_weight
            rounded = lax.optimization_barrier(diag_weight.astype(jnp.bfloat16)).astype(jnp.float32)
            diag_vals = lax.dynamic_slice_in_dim(pair[1], block_start, block_width, 0).astype(jnp.float32)
            accumulated = accumulated + rounded[..., None] * diag_vals[:, :, None, :]
        result = (accumulated / denominator[..., None]).astype(jnp.bfloat16)
        return result.reshape(block_width, HEADS * HD), row_peak.reshape(block_width, HEADS)

    blocks, peaks = lax.map(one_block, jnp.arange(TOKENS // block_width, dtype=jnp.int32))
    return blocks.reshape(TOKENS, HEADS * HD), peaks.reshape(TOKENS, HEADS)


def reference(queries, draft_kv, doc_ids, logits, targets):
    results = [attend_step(step_index, queries, draft_kv, doc_ids) for step_index in range(STEPS)]
    attended = jnp.stack([pair[0] for pair in results])
    row_peak = jnp.stack([pair[1] for pair in results])
    block_width = math.gcd(TOKENS, 512)

    def loss_block(block_index):
        block_start = block_index * block_width
        values = lax.dynamic_slice_in_dim(logits, block_start, block_width, 0).astype(jnp.float32)
        wanted = lax.dynamic_slice_in_dim(targets, block_start, block_width, 0)
        vocab_peak = jnp.max(values, axis=1)
        vocab_total = jnp.sum(jnp.exp(values - vocab_peak[:, None]), axis=1)
        columns = jnp.arange(VOCAB, dtype=jnp.int32)
        target_logit = jnp.sum(jnp.where(columns[None, :] == wanted[:, None], values, 0.0), axis=1)
        return vocab_peak + jnp.log(vocab_total) - target_logit

    token_loss = lax.map(loss_block, jnp.arange(TOKENS // block_width, dtype=jnp.int32)).reshape(TOKENS)
    return attended, row_peak, token_loss
```

```python
import functools

import jax
import jax.numpy as jnp
from jax import lax
from jax.experimental import pallas as pl
from jax.experimental.pallas import tpu as pltpu
from jax.sharding import PartitionSpec as P

HD = 128
STEPS = 3
TOK = 256
GROUP = 4
WINDOW = 24
KEYS = GROUP * TOK
HEADS = 8
VROWS = HD + 16
SCALE = HD ** (-0.5)
LOG2E = 1.4426950408889634
C = SCALE * LOG2E
BIG = 1e30
CHUNK = 256
f32, bf16 = jnp.float32, jnp.bfloat16
NT = (((1,), (1,)), ((), ()))
NN = (((1,), (0,)), ((), ()))
TN = (((0,), (0,)), ((), ()))
MESH = pl.DeviceIdType.MESH


def dg(a, b, dims):
    return lax.dot_general(a, b, dims, preferred_element_type=f32)


def as_column(row, rows=TOK):
    wide = jnp.broadcast_to(row, (16, rows)).astype(bf16)
    return dg(wide, jnp.full((16, HD), 1.0 / 16, bf16), TN)


def kernel(
    n_vocab, vocab_width,
    q_hbm, kv_ref, doc_ref, lg_hbm, tg_ref,
    out_ref, peak_ref, loss_ref,
    qv, lg, kall, vall, kd, vd, bias, gk, gv, sb, pb, bm, al, mx, acc, cols, packets, peaks,
    q_sem, lg_sem, send_sem, recv_sem, lsend_sem, lrecv_sem,
):
    me = lax.axis_index("seq")
    mv = lax.axis_index("vocab")
    z = me // 8
    x = (me // 2) % 4
    c = me % 2

    q_copy = pltpu.make_async_copy(q_hbm, qv, q_sem)
    n_lg = 4
    lg_rows = TOK // n_lg
    lg_copies = [
        pltpu.make_async_copy(
            lg_hbm.at[pl.ds(k * lg_rows, lg_rows)], lg.at[pl.ds(k * lg_rows, lg_rows)], lg_sem.at[k]
        )
        for k in range(n_lg)
    ]
    for copy in lg_copies:
        copy.start()
    q_copy.start()

    def dev(zz, xx, cc):
        return zz * 8 + xx * 2 + cc

    barrier = pltpu.get_barrier_semaphore()
    partners = [dev((z + d) % 4, x, c) for d in (1, 2, 3)]
    partners += [dev(z, (x + d) % 4, c) for d in (1, 2, 3)]
    partners += [dev(z, x, 1 - c)]
    for p in partners:
        pl.semaphore_signal(barrier, inc=1, device_id=(p, mv), device_id_type=MESH)
    for d in range(1, n_vocab):
        pl.semaphore_signal(
            barrier, inc=1, device_id=(me, lax.rem(mv + d, n_vocab)), device_id_type=MESH
        )

    docs = doc_ref[...].astype(f32)
    kall[me] = kv_ref[0, 0]
    vt = kv_ref[0, 1].astype(f32).T.astype(bf16)
    vall[me, 0:HD, :] = vt
    vall[me, HD:VROWS, :] = jnp.broadcast_to(docs, (16, TOK)).astype(bf16)

    pl.semaphore_wait(barrier, len(partners) + n_vocab - 1)

    sends = []

    def descriptors(block, target, slot):
        return [
            pltpu.make_async_remote_copy(
                src_ref=buf.at[block],
                dst_ref=buf.at[block],
                send_sem=send_sem.at[slot, k],
                recv_sem=recv_sem.at[block, k],
                device_id=(target, mv),
                device_id_type=MESH,
            )
            for k, buf in enumerate((kall, vall))
        ]

    def send(what):
        slot = len(sends)
        sends.append(what)
        cond, block, target = what()

        def go():
            for d in descriptors(block, target, slot):
                d.start()

        pl.when(cond)(go)

    def arrived(cond, block):
        def go():
            for d in descriptors(block, me, 0):
                d.wait_recv()

        pl.when(cond)(go)

    def wanted(dz, xx, at_x):
        if dz == 0:
            return xx < at_x
        if dz == 3:
            return (z >= 3) & (xx >= at_x)
        return z >= dz

    def plane_send(dz):
        return z + dz <= 3, me, dev(z + dz, x, c)

    def column_send(dz, d):
        xx = (x + d) % 4
        return wanted(dz, x, xx), dev(z - dz, x, c), dev(z, xx, c)

    def core_send(dz, d):
        xx = (x + d) % 4
        if d:
            cond = wanted(dz, xx, x)
        else:
            cond = z >= dz if dz else c == 0
        return cond, dev(z - dz, xx, c), dev(z, x, 1 - c)

    def forward_column(dz, arrive):
        if arrive:
            arrived(z >= dz, dev(z - dz, x, c))
        for d in (1, 3, 2):
            send(functools.partial(column_send, dz, d))
        send(functools.partial(core_send, dz, 0))

    def forward_row(dz):
        for d in (1, 3, 2):
            xx = (x + d) % 4
            block = dev(z - dz, xx, c)
            arrived(wanted(dz, xx, x), block)
            send(functools.partial(core_send, dz, d))

    def arrive_core(dz):
        for d in (0, 1, 3, 2):
            xx = (x + d) % 4
            if d:
                cond = wanted(dz, xx, x)
            else:
                cond = z >= dz if dz else c == 1
            arrived(cond, dev(z - dz, xx, 1 - c))

    for dz in (1, 2, 3):
        send(functools.partial(plane_send, dz))
    forward_column(0, False)

    target = tg_ref[...] - mv * vocab_width
    inside = (target >= 0) & (target < vocab_width)
    target = jnp.where(inside, target, 0)
    hi = target // 256
    lo = target - hi * 256
    tcol = as_column(hi.astype(f32)) * 256.0 + as_column(lo.astype(f32))
    tcol = jnp.where(as_column(inside.astype(f32)) > 0.5, tcol, -1.0)
    cols[...] = tcol
    LR, LC = 32, 512
    for copy in lg_copies:
        copy.wait()

    def loss_rows(k, _):
        rows = pl.ds(pl.multiple_of(k * LR, LR), LR)
        top = lg[rows, 0:LC]
        for ch in range(1, vocab_width // LC):
            top = jnp.maximum(top, lg[rows, ch * LC : (ch + 1) * LC])
        top = jnp.max(top.astype(f32), axis=1, keepdims=True)
        want = cols[rows, 0:1].astype(jnp.int32)
        lane = lax.broadcasted_iota(jnp.int32, (LR, LC), 1)
        total = jnp.zeros((LR, LC), f32)
        found = jnp.zeros((LR, LC), f32)
        for ch in range(vocab_width // LC):
            v = lg[rows, ch * LC : (ch + 1) * LC].astype(f32)
            total = total + jnp.exp(v - top)
            found = found + jnp.where(lane == want - ch * LC, v, 0.0)
        total = jnp.sum(total, axis=1, keepdims=True)
        found = jnp.sum(found, axis=1, keepdims=True)
        at = lax.broadcasted_iota(jnp.int32, (LR, HD), 1)
        cols[rows, :] = jnp.where(at == 0, top, jnp.where(at == 1, total, found))
        return 0

    lax.fori_loop(0, TOK // LR, loss_rows, 0)
    packets[mv] = cols[...].T[0:8, :]

    def loss_copy(d):
        other = lax.rem(mv + d, n_vocab)
        return pltpu.make_async_remote_copy(
            src_ref=packets.at[mv],
            dst_ref=packets.at[mv],
            send_sem=lsend_sem.at[d],
            recv_sem=lrecv_sem.at[mv],
            device_id=(me, other),
            device_id_type=MESH,
        )

    for d in range(1, n_vocab):
        loss_copy(d).start()

    forward_column(1, True)
    forward_row(0)

    dcol = as_column(docs)
    key_at = lax.broadcasted_iota(jnp.int32, (TOK, TOK), 0)
    row_at = lax.broadcasted_iota(jnp.int32, (TOK, TOK), 1)
    usable = (key_at <= row_at) & (dcol[:, 0:1] == docs)
    bias[0] = jnp.where(usable, 0.0, -BIG)
    bias[1] = jnp.where(key_at == row_at, 0.0, -BIG)
    ones = jnp.ones((16, TOK), bf16)
    for s in range(STEPS):
        kd[s * TOK : (s + 1) * TOK, :] = kv_ref[s, 0]
        vd[0:HD, s * TOK : (s + 1) * TOK] = vt if s == 0 else kv_ref[s, 1].astype(f32).T.astype(bf16)
        vd[HD:VROWS, s * TOK : (s + 1) * TOK] = ones
    q_copy.wait()

    def diag_scores(s, h, slot):
        parts = []
        for k in range(s + 1):
            sc = dg(kd[k * TOK : (k + 1) * TOK, :], qv[s, :, h * HD : (h + 1) * HD], NT)
            sc = sc + bias[min(k, 1)]
            sb[slot, k * TOK : (k + 1) * TOK] = sc
            parts.append(jnp.max(sc.reshape(TOK // 8, 8, TOK), axis=0))
        bm[slot] = jnp.max(functools.reduce(jnp.maximum, parts), axis=0, keepdims=True)

    def diag_values(s, h, slot):
        tile = s * HEADS + h
        mx[tile] = bm[slot]
        mc = bm[slot] * C
        n = (s + 1) * TOK
        for k in range(s + 1):
            at = slice(k * TOK, (k + 1) * TOK)
            pb[slot, at] = jnp.exp2(sb[slot, at] * C - mc).astype(bf16)
        acc[tile] = dg(vd[:, 0:n], pb[slot, 0:n], NN)

    order = [(s, h) for s in range(STEPS) for h in range(HEADS)]
    diag_scores(*order[0], 0)
    for k, (s, h) in enumerate(order):
        if k + 1 < len(order):
            diag_scores(*order[k + 1], (k + 1) % 2)
        diag_values(s, h, k % 2)

    forward_column(2, True)
    forward_row(1)
    arrive_core(0)
    arrive_core(1)
    groups = (jnp.minimum(me, WINDOW) + GROUP - 1) // GROUP
    first_doc = docs[:, 0:1]
    row_ok = docs == first_doc
    first_key = kv_ref[0, 0, 0:1, :].astype(f32)

    def prepare(g):
        buf = g % 2
        for k in range(GROUP):
            block = me - GROUP * (g + 1) + k
            at = jnp.maximum(block, 0)
            known = jnp.where(block >= 0, 1.0, 0.0)
            mask = jnp.where(vall[at, HD:VROWS, :].astype(f32) == first_doc, 1.0, 0.0) * known
            keep = dg(mask.astype(bf16), jnp.ones((16, HD), bf16), TN) > 0.5
            gk[buf, k * TOK : (k + 1) * TOK, :] = jnp.where(
                keep, kall[at].astype(f32), first_key
            ).astype(bf16)
            gv[buf, 0:HD, k * TOK : (k + 1) * TOK] = jnp.where(
                mask[0:1] > 0.5, vall[at, 0:HD, :].astype(f32), 0.0
            ).astype(bf16)
            gv[buf, HD:VROWS, k * TOK : (k + 1) * TOK] = mask.astype(bf16)

    def scores(buf, s, h, slot):
        parts = []
        for k in range(KEYS // CHUNK):
            at = slice(k * CHUNK, (k + 1) * CHUNK)
            sc = dg(gk[buf, at, :], qv[s, :, h * HD : (h + 1) * HD], NT)
            sb[slot, at] = sc
            parts.append(jnp.max(sc.reshape(CHUNK // 8, 8, TOK), axis=0))
        bm[slot] = jnp.max(functools.reduce(jnp.maximum, parts), axis=0, keepdims=True)

    def values(buf, s, h, slot):
        tile = s * HEADS + h
        old = mx[tile]
        new = jnp.where(row_ok, jnp.maximum(old, bm[slot]), old)
        mx[tile] = new
        alpha = jnp.exp2((old - new) * C)
        mc = jnp.where(row_ok, new * C, BIG)
        for k in range(KEYS // CHUNK):
            at = slice(k * CHUNK, (k + 1) * CHUNK)
            pb[slot, at] = jnp.exp2(sb[slot, at] * C - mc).astype(bf16)
        acc[tile] = acc[tile] * alpha + dg(gv[buf], pb[slot], NN)

    prepare(0)
    scores(0, 0, 0, 0)
    last = groups * STEPS - 1

    def body(t, _):
        g, s = t // STEPS, t % STEPS
        ahead = jnp.minimum(t + 1, last)
        g_next, s_next = ahead // STEPS, ahead % STEPS

        @pl.when(t == 0)
        def _():
            forward_column(3, True)

        @pl.when(t == 2)
        def _():
            forward_row(2)

        @pl.when(t == 4)
        def _():
            arrive_core(2)

        @pl.when(t == 7)
        def _():
            forward_row(3)

        @pl.when(t == 9)
        def _():
            arrive_core(3)

        @pl.when((s == 1) & (g + 1 < groups))
        def _():
            prepare(g + 1)

        for h in range(HEADS):
            if h + 1 < HEADS:
                scores(g % 2, s, h + 1, (h + 1) % 2)
            else:
                scores(g_next % 2, s_next, 0, 0)
            values(g % 2, s, h, h % 2)
        return 0

    lax.fori_loop(0, groups * STEPS, body, 0)

    def finish(s, _):
        for h in range(HEADS):
            tile = s * HEADS + h
            share = 1.0 / acc[tile, HD : HD + 1, :]
            out_ref[s, :, h * HD : (h + 1) * HD] = (acc[tile, 0:HD, :] * share).T.astype(bf16)
        return 0

    lax.fori_loop(0, STEPS, finish, 0)
    for k in range(STEPS * HEADS):
        peaks[k : k + 1, :] = mx[k] * SCALE
    turned = peaks[...].T
    for s in range(STEPS):
        peak_ref[s] = turned[:, s * HEADS : (s + 1) * HEADS]

    for d in range(1, n_vocab):
        other = lax.rem(mv + n_vocab - d, n_vocab)
        pltpu.make_async_remote_copy(
            src_ref=packets.at[other],
            dst_ref=packets.at[other],
            send_sem=lsend_sem.at[d],
            recv_sem=lrecv_sem.at[other],
            device_id=(me, other),
            device_id_type=MESH,
        ).wait_recv()
    top = packets[0, 0:1, :]
    for k in range(1, n_vocab):
        top = jnp.maximum(top, packets[k, 0:1, :])
    total = jnp.zeros_like(top)
    found = jnp.zeros_like(top)
    for k in range(n_vocab):
        total = total + packets[k, 1:2, :] * jnp.exp(packets[k, 0:1, :] - top)
        found = found + packets[k, 2:3, :]
    loss_ref[...] = top + jnp.log(total) - found

    for d in range(1, n_vocab):
        loss_copy(d).wait_send()
    for slot, what in enumerate(sends):
        cond, block, target = what()

        def left(block=block, target=target, slot=slot):
            for d in descriptors(block, target, slot):
                d.wait_send()

        pl.when(cond)(left)


def local(n_vocab, queries, draft_kv, doc_ids, logits, targets):
    vocab_width = logits.shape[1]
    any_spec = pl.BlockSpec(memory_space=pl.ANY)
    vmem = pl.BlockSpec(memory_space=pltpu.VMEM)
    out = pl.pallas_call(
        functools.partial(kernel, n_vocab, vocab_width),
        out_shape=[
            jax.ShapeDtypeStruct(queries.shape, bf16),
            jax.ShapeDtypeStruct((STEPS, TOK, HEADS), f32),
            jax.ShapeDtypeStruct((1, TOK), f32),
        ],
        in_specs=[any_spec, vmem, vmem, any_spec, vmem],
        out_specs=[vmem, vmem, vmem],
        scratch_shapes=[
            pltpu.VMEM(queries.shape, bf16),
            pltpu.VMEM(logits.shape, bf16),
            pltpu.VMEM((32, TOK, HD), bf16),
            pltpu.VMEM((32, VROWS, TOK), bf16),
            pltpu.VMEM((STEPS * TOK, HD), bf16),
            pltpu.VMEM((VROWS, STEPS * TOK), bf16),
            pltpu.VMEM((2, TOK, TOK), f32),
            pltpu.VMEM((2, KEYS, HD), bf16),
            pltpu.VMEM((2, VROWS, KEYS), bf16),
            pltpu.VMEM((2, KEYS, TOK), f32),
            pltpu.VMEM((2, KEYS, TOK), bf16),
            pltpu.VMEM((2, 1, TOK), f32),
            pltpu.VMEM((2, 1, TOK), f32),
            pltpu.VMEM((STEPS * HEADS, 1, TOK), f32),
            pltpu.VMEM((STEPS * HEADS, VROWS, TOK), f32),
            pltpu.VMEM((TOK, HD), f32),
            pltpu.VMEM((n_vocab, 8, TOK), f32),
            pltpu.VMEM((HD, TOK), f32),
            pltpu.SemaphoreType.DMA,
            pltpu.SemaphoreType.DMA((4,)),
            pltpu.SemaphoreType.DMA((32, 2)),
            pltpu.SemaphoreType.DMA((32, 2)),
            pltpu.SemaphoreType.DMA((n_vocab,)),
            pltpu.SemaphoreType.DMA((n_vocab,)),
        ],
        compiler_params=pltpu.CompilerParams(
            collective_id=0, has_side_effects=True, vmem_limit_bytes=48 * 2**20
        ),
        cost_estimate=pl.CostEstimate(
            flops=20 * 10**9, bytes_accessed=10 * 2**20, transcendentals=40 * 10**6
        ),
    )(queries, draft_kv, doc_ids.reshape(1, TOK), logits, targets.reshape(1, TOK))
    return out[0], out[1], out[2].reshape(TOK)


def solution(mesh):
    in_specs = (
        P(None, "seq", "vocab"),
        P(None, None, "seq", "vocab"),
        P("seq"),
        P("seq", "vocab"),
        P("seq"),
    )
    out_specs = (P(None, "seq", "vocab"), P(None, "seq", "vocab"), P("seq"))
    step = functools.partial(local, mesh.shape["vocab"])
    return jax.shard_map(step, mesh=mesh, in_specs=in_specs, out_specs=out_specs, check_vma=False)
```

```python
import functools

import jax
import jax.numpy as jnp
from jax import lax
from jax.experimental import pallas as pl
from jax.experimental.pallas import tpu as pltpu
from jax.sharding import PartitionSpec as P

HD = 128
STEPS = 3
TOK = 256
GROUP = 6
WINDOW = 24
KEYS = GROUP * TOK
HEADS = 8
VROWS = HD + 16
SCALE = HD ** (-0.5)
LOG2E = 1.4426950408889634
C = SCALE * LOG2E
BIG = 1e30
CHUNK = 256
f32, bf16 = jnp.float32, jnp.bfloat16
NT = (((1,), (1,)), ((), ()))
NN = (((1,), (0,)), ((), ()))
TN = (((0,), (0,)), ((), ()))
MESH = pl.DeviceIdType.MESH


def dg(a, b, dims):
    return lax.dot_general(a, b, dims, preferred_element_type=f32)


def as_column(row, rows=TOK):
    wide = jnp.broadcast_to(row, (16, rows)).astype(bf16)
    return dg(wide, jnp.full((16, HD), 1.0 / 16, bf16), TN)


def kernel(
    n_vocab, vocab_width,
    q_hbm, kv_hbm, doc_hbm, lg_hbm, tg_hbm,
    out_ref, peak_ref, loss_ref,
    qv, kv_ref, doc_ref, tg_ref, lg, kall, vall, kd, vd, bias, gk, gv, sb, pb, bm, al, mx, acc, cols, packets,
    in_sem, lg_sem, send_sem, recv_sem, lsend_sem, lrecv_sem,
):
    me = lax.axis_index("seq")
    mv = lax.axis_index("vocab")
    z = me // 8
    x = (me // 2) % 4
    c = me % 2
    near = me % 8 < 2

    in_copies = [
        pltpu.make_async_copy(src, dst, in_sem.at[k])
        for k, (src, dst) in enumerate(
            ((kv_hbm, kv_ref), (doc_hbm, doc_ref), (tg_hbm, tg_ref))
        )
    ]
    in_copies += [
        pltpu.make_async_copy(
            q_hbm.at[:, :, pl.ds(h * HD, HD)], qv.at[h], in_sem.at[3 + h]
        )
        for h in range(HEADS)
    ]
    for copy in in_copies[:3]:
        copy.start()
    n_lg = 4
    lg_rows = TOK // n_lg
    lg_copies = [
        pltpu.make_async_copy(
            lg_hbm.at[pl.ds(k * lg_rows, lg_rows)], lg.at[pl.ds(k * lg_rows, lg_rows)], lg_sem.at[k]
        )
        for k in range(n_lg)
    ]
    for copy in lg_copies:
        copy.start()
    for copy in in_copies[3:]:
        copy.start()

    def dev(zz, xx, cc):
        return zz * 8 + xx * 2 + cc

    barrier = pltpu.get_barrier_semaphore()
    partners = [dev((z + d) % 4, x, c) for d in (1, 2, 3)]
    partners += [dev(z, (x + d) % 4, c) for d in (1, 2, 3)]
    partners += [dev(z, x, 1 - c)]
    for p in partners:
        pl.semaphore_signal(barrier, inc=1, device_id=(p, mv), device_id_type=MESH)
    for d in range(1, n_vocab):
        pl.semaphore_signal(
            barrier, inc=1, device_id=(me, lax.rem(mv + d, n_vocab)), device_id_type=MESH
        )

    for copy in in_copies[:3]:
        copy.wait()
    docs = doc_ref[...].astype(f32)
    kall[me] = kv_ref[0, 0]
    vt = kv_ref[0, 1].astype(f32).T.astype(bf16)
    vall[me, 0:HD, :] = vt
    vall[me, HD:VROWS, :] = jnp.broadcast_to(docs, (16, TOK)).astype(bf16)

    pl.semaphore_wait(barrier, len(partners) + n_vocab - 1)

    sends = []

    def descriptors(block, target, slot):
        return [
            pltpu.make_async_remote_copy(
                src_ref=buf.at[block],
                dst_ref=buf.at[block],
                send_sem=send_sem.at[slot, k],
                recv_sem=recv_sem.at[block, k],
                device_id=(target, mv),
                device_id_type=MESH,
            )
            for k, buf in enumerate((kall, vall))
        ]

    def send(what):
        slot = len(sends)
        sends.append(what)
        cond, block, target = what()

        def go():
            for d in descriptors(block, target, slot):
                d.start()

        pl.when(cond)(go)

    def arrived(cond, block):
        def go():
            for d in descriptors(block, me, 0):
                d.wait_recv()

        pl.when(cond)(go)

    def wanted(dz, xx, at_x):
        if dz == 0:
            return xx < at_x
        if dz == 3:
            return (z >= 3) & (xx >= at_x)
        return z >= dz

    def plane_send(dz):
        return z + dz <= 3, me, dev(z + dz, x, c)

    def column_send(dz, d):
        xx = (x + d) % 4
        return wanted(dz, x, xx), dev(z - dz, x, c), dev(z, xx, c)

    def core_send(dz, d):
        xx = (x + d) % 4
        if d:
            cond = wanted(dz, xx, x)
        else:
            cond = z >= dz if dz else c == 0
        return cond, dev(z - dz, xx, c), dev(z, x, 1 - c)

    def forward_column(dz, arrive):
        if arrive:
            arrived(z >= dz, dev(z - dz, x, c))
        for d in (1, 3, 2):
            send(functools.partial(column_send, dz, d))
        send(functools.partial(core_send, dz, 0))

    def forward_row(dz):
        for d in (1, 3, 2):
            xx = (x + d) % 4
            block = dev(z - dz, xx, c)
            arrived(wanted(dz, xx, x), block)
            send(functools.partial(core_send, dz, d))

    def arrive_core(dz, these=None):
        for d in (0, 1, 3, 2):
            xx = (x + d) % 4
            if d:
                cond = wanted(dz, xx, x)
            else:
                cond = z >= dz if dz else c == 1
            arrived(cond if these is None else cond & these, dev(z - dz, xx, 1 - c))

    for dz in (1, 2, 3):
        send(functools.partial(plane_send, dz))
    forward_column(0, False)

    target = tg_ref[...] - mv * vocab_width
    inside = (target >= 0) & (target < vocab_width)
    target = jnp.where(inside, target, 0)
    hi = target // 256
    lo = target - hi * 256
    tcol = as_column(hi.astype(f32)) * 256.0 + as_column(lo.astype(f32))
    tcol = jnp.where(as_column(inside.astype(f32)) > 0.5, tcol, -1.0)
    cols[...] = tcol
    LR, LC = 32, 512
    for copy in lg_copies:
        copy.wait()

    def loss_rows(k, _):
        rows = pl.ds(pl.multiple_of(k * LR, LR), LR)
        top = lg[rows, 0:LC]
        for ch in range(1, vocab_width // LC):
            top = jnp.maximum(top, lg[rows, ch * LC : (ch + 1) * LC])
        top = jnp.max(top.astype(f32), axis=1, keepdims=True)
        want = cols[rows, 0:1].astype(jnp.int32)
        lane = lax.broadcasted_iota(jnp.int32, (LR, LC), 1)
        total = jnp.zeros((LR, LC), f32)
        found = jnp.zeros((LR, LC), f32)
        for ch in range(vocab_width // LC):
            v = lg[rows, ch * LC : (ch + 1) * LC].astype(f32)
            total = total + jnp.exp(v - top)
            found = found + jnp.where(lane == want - ch * LC, v, 0.0)
        total = jnp.sum(total, axis=1, keepdims=True)
        found = jnp.sum(found, axis=1, keepdims=True)
        at = lax.broadcasted_iota(jnp.int32, (LR, HD), 1)
        cols[rows, :] = jnp.where(at == 0, top, jnp.where(at == 1, total, found))
        return 0

    lax.fori_loop(0, TOK // LR, loss_rows, 0)
    packets[mv] = cols[...].T[0:8, :]

    def loss_copy(d):
        other = lax.rem(mv + d, n_vocab)
        return pltpu.make_async_remote_copy(
            src_ref=packets.at[mv],
            dst_ref=packets.at[mv],
            send_sem=lsend_sem.at[d],
            recv_sem=lrecv_sem.at[mv],
            device_id=(me, other),
            device_id_type=MESH,
        )

    for d in range(1, n_vocab):
        loss_copy(d).start()

    forward_column(1, True)
    forward_row(0)

    dcol = as_column(docs)
    key_at = lax.broadcasted_iota(jnp.int32, (TOK, TOK), 0)
    row_at = lax.broadcasted_iota(jnp.int32, (TOK, TOK), 1)
    usable = (key_at <= row_at) & (dcol[:, 0:1] == docs)
    bias[0] = jnp.where(usable, 0.0, -BIG)
    bias[1] = jnp.where(key_at == row_at, 0.0, -BIG)
    ones = jnp.ones((16, TOK), bf16)
    for s in range(STEPS):
        kd[s * TOK : (s + 1) * TOK, :] = kv_ref[s, 0]
        vd[0:HD, s * TOK : (s + 1) * TOK] = vt if s == 0 else kv_ref[s, 1].astype(f32).T.astype(bf16)
        vd[HD:VROWS, s * TOK : (s + 1) * TOK] = ones
    for copy in in_copies[3:]:
        copy.wait()

    def diag_scores(s, h, slot):
        parts = []
        for k in range(s + 1):
            sc = dg(kd[k * TOK : (k + 1) * TOK, :], qv[h, s], NT)
            sc = sc + bias[min(k, 1)]
            sb[slot, k * TOK : (k + 1) * TOK] = sc
            parts.append(jnp.max(sc.reshape(TOK // 8, 8, TOK), axis=0))
        bm[slot] = jnp.max(functools.reduce(jnp.maximum, parts), axis=0, keepdims=True)

    def diag_values(s, h, slot):
        tile = s * HEADS + h
        mx[tile] = bm[slot]
        mc = bm[slot] * C
        n = (s + 1) * TOK
        for k in range(s + 1):
            at = slice(k * TOK, (k + 1) * TOK)
            pb[slot, at] = jnp.exp2(sb[slot, at] * C - mc).astype(bf16)
        acc[tile] = dg(vd[:, 0:n], pb[slot, 0:n], NN)

    for s in range(STEPS):
        diag_scores(s, 0, 0)
        for h in range(HEADS):
            if h + 1 < HEADS:
                diag_scores(s, h + 1, (h + 1) % 2)
            diag_values(s, h, h % 2)
        if s == 1:
            forward_column(2, True)

    forward_row(1)
    arrive_core(0)
    arrive_core(1)
    groups = (jnp.minimum(me, WINDOW) + GROUP - 1) // GROUP
    first_doc = docs[:, 0:1]
    row_ok = docs == first_doc
    first_key = kv_ref[0, 0, 0:1, :]

    def prepare(g, buf, first, count):
        base = me - GROUP * (g + 1) + first
        at = [jnp.maximum(base + k, 0) for k in range(count)]
        masks = []
        for k in range(count):
            known = jnp.where(base + k >= 0, 1.0, 0.0)
            same = vall[at[k], HD:VROWS, :].astype(f32) == first_doc
            masks.append((jnp.where(same, 1.0, 0.0) * known).astype(bf16))
        mask = jnp.concatenate(masks, axis=1)
        keep = dg(mask, jnp.full((16, HD), 1.0 / 16, bf16), TN).astype(bf16)
        for k in range(count):
            gv[buf, first + k, HD:VROWS, :] = masks[k]
            gv[buf, first + k, 0:HD, :] = vall[at[k], 0:HD, :] * masks[k][0:1]
            part = keep[k * TOK : (k + 1) * TOK]
            gk[buf, first + k] = kall[at[k]] * part + first_key * (1.0 - part)

    def scores(buf, s, h, slot):
        parts = []
        for k in range(GROUP):
            at = slice(k * TOK, (k + 1) * TOK)
            sc = dg(gk[buf, k], qv[h, s], NT)
            sb[slot, at] = sc
            parts.append(jnp.max(sc.reshape(TOK // 8, 8, TOK), axis=0))
        bm[slot] = jnp.max(functools.reduce(jnp.maximum, parts), axis=0, keepdims=True)

    def values(buf, s, h, slot):
        tile = s * HEADS + h
        old = mx[tile]
        new = jnp.where(row_ok, jnp.maximum(old, bm[slot]), old)
        mx[tile] = new
        alpha = jnp.exp2((old - new) * C)
        mc = jnp.where(row_ok, new * C, BIG)
        for k in range(KEYS // CHUNK):
            at = slice(k * CHUNK, (k + 1) * CHUNK)
            pb[slot, at] = jnp.exp2(sb[slot, at] * C - mc).astype(bf16)
        gvw = jnp.concatenate([gv[buf, k] for k in range(GROUP)], axis=1)
        acc[tile] = acc[tile] * alpha + dg(gvw, pb[slot], NN)

    prepare(0, 0, 0, GROUP)
    scores(0, 0, 0, 0)
    last = groups * STEPS - 1

    def body(t, _):
        g, s = t // STEPS, t % STEPS
        ahead = jnp.minimum(t + 1, last)
        g_next, s_next = ahead // STEPS, ahead % STEPS

        @pl.when(t == 0)
        def _():
            forward_column(3, True)

        @pl.when(t == 1)
        def _():
            forward_row(2)
            arrive_core(2, near)

        @pl.when(t == 2)
        def _():
            arrive_core(2, ~near)

        @pl.when(t == 3)
        def _():
            forward_row(3)

        @pl.when(t == 5)
        def _():
            arrive_core(3)

        prepare(jnp.minimum(g + 1, groups - 1), (g + 1) % 2, GROUP - 2 - 2 * s, 2)

        for h in range(HEADS):
            if h + 1 < HEADS:
                scores(g % 2, s, h + 1, (h + 1) % 2)
            else:
                scores(g_next % 2, s_next, 0, 0)
            values(g % 2, s, h, h % 2)
        return 0

    lax.fori_loop(0, groups * STEPS, body, 0)

    def finish(s, _):
        for h in range(HEADS):
            tile = s * HEADS + h
            share = 1.0 / acc[tile, HD : HD + 1, :]
            out_ref[s, :, h * HD : (h + 1) * HD] = (acc[tile, 0:HD, :] * share).T.astype(bf16)
        return 0

    lax.fori_loop(0, STEPS, finish, 0)
    for k in range(STEPS * HEADS):
        peak_ref[k // HEADS, k % HEADS : k % HEADS + 1, :] = mx[k] * SCALE

    for d in range(1, n_vocab):
        other = lax.rem(mv + n_vocab - d, n_vocab)
        pltpu.make_async_remote_copy(
            src_ref=packets.at[other],
            dst_ref=packets.at[other],
            send_sem=lsend_sem.at[d],
            recv_sem=lrecv_sem.at[other],
            device_id=(me, other),
            device_id_type=MESH,
        ).wait_recv()
    top = packets[0, 0:1, :]
    for k in range(1, n_vocab):
        top = jnp.maximum(top, packets[k, 0:1, :])
    total = jnp.zeros_like(top)
    found = jnp.zeros_like(top)
    for k in range(n_vocab):
        total = total + packets[k, 1:2, :] * jnp.exp(packets[k, 0:1, :] - top)
        found = found + packets[k, 2:3, :]
    loss_ref[...] = top + jnp.log(total) - found

    for d in range(1, n_vocab):
        loss_copy(d).wait_send()
    for slot, what in enumerate(sends):
        cond, block, target = what()

        def left(block=block, target=target, slot=slot):
            for d in descriptors(block, target, slot):
                d.wait_send()

        pl.when(cond)(left)


def local(n_vocab, queries, draft_kv, doc_ids, logits, targets):
    vocab_width = logits.shape[1]
    hbm = pl.BlockSpec(memory_space=pltpu.HBM)
    vmem = pl.BlockSpec(memory_space=pltpu.VMEM)
    out = pl.pallas_call(
        functools.partial(kernel, n_vocab, vocab_width),
        out_shape=[
            jax.ShapeDtypeStruct(queries.shape, bf16),
            jax.ShapeDtypeStruct((STEPS, HEADS, TOK), f32),
            jax.ShapeDtypeStruct((1, TOK), f32),
        ],
        in_specs=[hbm] * 5,
        out_specs=[vmem, vmem, vmem],
        scratch_shapes=[
            pltpu.VMEM((HEADS, STEPS, TOK, HD), bf16),
            pltpu.VMEM(draft_kv.shape, bf16),
            pltpu.VMEM((1, TOK), jnp.int32),
            pltpu.VMEM((1, TOK), jnp.int32),
            pltpu.VMEM(logits.shape, bf16),
            pltpu.VMEM((32, TOK, HD), bf16),
            pltpu.VMEM((32, VROWS, TOK), bf16),
            pltpu.VMEM((STEPS * TOK, HD), bf16),
            pltpu.VMEM((VROWS, STEPS * TOK), bf16),
            pltpu.VMEM((2, TOK, TOK), f32),
            pltpu.VMEM((2, GROUP, TOK, HD), bf16),
            pltpu.VMEM((2, GROUP, VROWS, TOK), bf16),
            pltpu.VMEM((2, KEYS, TOK), f32),
            pltpu.VMEM((2, KEYS, TOK), bf16),
            pltpu.VMEM((2, 1, TOK), f32),
            pltpu.VMEM((2, 1, TOK), f32),
            pltpu.VMEM((STEPS * HEADS, 1, TOK), f32),
            pltpu.VMEM((STEPS * HEADS, VROWS, TOK), f32),
            pltpu.VMEM((TOK, HD), f32),
            pltpu.VMEM((n_vocab, 8, TOK), f32),
            pltpu.SemaphoreType.DMA((3 + HEADS,)),
            pltpu.SemaphoreType.DMA((4,)),
            pltpu.SemaphoreType.DMA((32, 2)),
            pltpu.SemaphoreType.DMA((32, 2)),
            pltpu.SemaphoreType.DMA((n_vocab,)),
            pltpu.SemaphoreType.DMA((n_vocab,)),
        ],
        compiler_params=pltpu.CompilerParams(
            collective_id=0, has_side_effects=True, vmem_limit_bytes=64 * 2**20
        ),
        cost_estimate=pl.CostEstimate(
            flops=20 * 10**9, bytes_accessed=10 * 2**20, transcendentals=40 * 10**6
        ),
    )(queries, draft_kv, doc_ids.reshape(1, TOK), logits, targets.reshape(1, TOK))
    return out[0], out[1].transpose(0, 2, 1), out[2].reshape(TOK)


def solution(mesh):
    in_specs = (
        P(None, "seq", "vocab"),
        P(None, None, "seq", "vocab"),
        P("seq"),
        P("seq", "vocab"),
        P("seq"),
    )
    out_specs = (P(None, "seq", "vocab"), P(None, "seq", "vocab"), P("seq"))
    step = functools.partial(local, mesh.shape["vocab"])
    return jax.shard_map(step, mesh=mesh, in_specs=in_specs, out_specs=out_specs, check_vma=False)
```

```python
import functools

import jax
import jax.numpy as jnp
from jax import lax
from jax.experimental import pallas as pl
from jax.experimental.pallas import tpu as pltpu
from jax.sharding import PartitionSpec as P

HD = 128
STEPS = 3
TOK = 256
GROUP = 6
WINDOW = 24
KEYS = GROUP * TOK
HEADS = 8
VROWS = HD + 16
SCALE = HD ** (-0.5)
LOG2E = 1.4426950408889634
C = SCALE * LOG2E
BIG = 1e30
f32, bf16 = jnp.float32, jnp.bfloat16
NT = (((1,), (1,)), ((), ()))
NN = (((1,), (0,)), ((), ()))
TN = (((0,), (0,)), ((), ()))
MESH = pl.DeviceIdType.MESH


def dg(a, b, dims):
    return lax.dot_general(a, b, dims, preferred_element_type=f32)


def as_column(row, rows=TOK):
    wide = jnp.broadcast_to(row, (16, rows)).astype(bf16)
    return dg(wide, jnp.full((16, HD), 1.0 / 16, bf16), TN)


def kernel(
    n_vocab, vocab_width,
    q_hbm, kv_hbm, doc_hbm, lg_hbm, tg_hbm,
    out_ref, peak_ref, loss_ref,
    qv, kv_ref, doc_ref, tg_ref, lg, kall, vall, kd, vd, bias, gk, gv, sb, pb, bm, al, mx, acc, cols, packets,
    in_sem, lg_sem, send_sem, recv_sem, lsend_sem, lrecv_sem,
):
    me = lax.axis_index("seq")
    mv = lax.axis_index("vocab")
    z = me // 8
    x = (me // 2) % 4
    c = me % 2
    near = me % 8 < 2

    in_copies = [
        pltpu.make_async_copy(src, dst, in_sem.at[k])
        for k, (src, dst) in enumerate(
            ((kv_hbm, kv_ref), (doc_hbm, doc_ref), (tg_hbm, tg_ref))
        )
    ]
    in_copies += [
        pltpu.make_async_copy(
            q_hbm.at[:, :, pl.ds(h * HD, HD)], qv.at[h], in_sem.at[3 + h]
        )
        for h in range(HEADS)
    ]
    for copy in in_copies[:3]:
        copy.start()
    n_lg = 4
    lg_rows = TOK // n_lg
    lg_copies = [
        pltpu.make_async_copy(
            lg_hbm.at[pl.ds(k * lg_rows, lg_rows)], lg.at[pl.ds(k * lg_rows, lg_rows)], lg_sem.at[k]
        )
        for k in range(n_lg)
    ]
    for copy in lg_copies:
        copy.start()
    for copy in in_copies[3:]:
        copy.start()

    def dev(zz, xx, cc):
        return zz * 8 + xx * 2 + cc

    barrier = pltpu.get_barrier_semaphore()
    partners = [dev((z + d) % 4, x, c) for d in (1, 2, 3)]
    partners += [dev(z, (x + d) % 4, c) for d in (1, 2, 3)]
    partners += [dev(z, x, 1 - c)]
    for p in partners:
        pl.semaphore_signal(barrier, inc=1, device_id=(p, mv), device_id_type=MESH)
    for d in range(1, n_vocab):
        pl.semaphore_signal(
            barrier, inc=1, device_id=(me, lax.rem(mv + d, n_vocab)), device_id_type=MESH
        )

    for copy in in_copies[:3]:
        copy.wait()
    docs = doc_ref[...].astype(f32)
    kall[me] = kv_ref[0, 0]
    vt = kv_ref[0, 1].astype(f32).T.astype(bf16)
    vall[me, 0:HD, :] = vt
    vall[me, HD:VROWS, :] = jnp.broadcast_to(docs, (16, TOK)).astype(bf16)

    pl.semaphore_wait(barrier, len(partners) + n_vocab - 1)

    sends = []

    def descriptors(block, target, slot):
        return [
            pltpu.make_async_remote_copy(
                src_ref=buf.at[block],
                dst_ref=buf.at[block],
                send_sem=send_sem.at[slot, k],
                recv_sem=recv_sem.at[block, k],
                device_id=(target, mv),
                device_id_type=MESH,
            )
            for k, buf in enumerate((kall, vall))
        ]

    def send(what):
        slot = len(sends)
        sends.append(what)
        cond, block, target = what()

        def go():
            for d in descriptors(block, target, slot):
                d.start()

        pl.when(cond)(go)

    def arrived(cond, block):
        def go():
            for d in descriptors(block, me, 0):
                d.wait_recv()

        pl.when(cond)(go)

    def wanted(dz, xx, at_x):
        if dz == 0:
            return xx < at_x
        if dz == 3:
            return (z >= 3) & (xx >= at_x)
        return z >= dz

    def plane_send(dz):
        return z + dz <= 3, me, dev(z + dz, x, c)

    def column_send(dz, d):
        xx = (x + d) % 4
        return wanted(dz, x, xx), dev(z - dz, x, c), dev(z, xx, c)

    def core_send(dz, d):
        xx = (x + d) % 4
        if d:
            cond = wanted(dz, xx, x)
        else:
            cond = z >= dz if dz else c == 0
        return cond, dev(z - dz, xx, c), dev(z, x, 1 - c)

    def forward_column(dz, arrive):
        if arrive:
            arrived(z >= dz, dev(z - dz, x, c))
        for d in (1, 3, 2):
            send(functools.partial(column_send, dz, d))
        send(functools.partial(core_send, dz, 0))

    def forward_row(dz):
        for d in (1, 3, 2):
            xx = (x + d) % 4
            block = dev(z - dz, xx, c)
            arrived(wanted(dz, xx, x), block)
            send(functools.partial(core_send, dz, d))

    def arrive_core(dz, these=None):
        for d in (0, 1, 3, 2):
            xx = (x + d) % 4
            if d:
                cond = wanted(dz, xx, x)
            else:
                cond = z >= dz if dz else c == 1
            arrived(cond if these is None else cond & these, dev(z - dz, xx, 1 - c))

    for dz in (1, 2, 3):
        send(functools.partial(plane_send, dz))
    forward_column(0, False)

    target = tg_ref[...] - mv * vocab_width
    inside = (target >= 0) & (target < vocab_width)
    target = jnp.where(inside, target, 0)
    hi = target // 256
    lo = target - hi * 256
    tcol = as_column(hi.astype(f32)) * 256.0 + as_column(lo.astype(f32))
    tcol = jnp.where(as_column(inside.astype(f32)) > 0.5, tcol, -1.0)
    cols[...] = tcol
    LR, LC = 32, 512
    for copy in lg_copies:
        copy.wait()

    def loss_rows(k, _):
        rows = pl.ds(pl.multiple_of(k * LR, LR), LR)
        top = lg[rows, 0:LC]
        for ch in range(1, vocab_width // LC):
            top = jnp.maximum(top, lg[rows, ch * LC : (ch + 1) * LC])
        top = jnp.max(top.astype(f32), axis=1, keepdims=True)
        want = cols[rows, 0:1].astype(jnp.int32)
        lane = lax.broadcasted_iota(jnp.int32, (LR, LC), 1)
        total = jnp.zeros((LR, LC), f32)
        found = jnp.zeros((LR, LC), f32)
        for ch in range(vocab_width // LC):
            v = lg[rows, ch * LC : (ch + 1) * LC].astype(f32)
            total = total + jnp.exp(v - top)
            found = found + jnp.where(lane == want - ch * LC, v, 0.0)
        total = jnp.sum(total, axis=1, keepdims=True)
        found = jnp.sum(found, axis=1, keepdims=True)
        at = lax.broadcasted_iota(jnp.int32, (LR, HD), 1)
        cols[rows, :] = jnp.where(at == 0, top, jnp.where(at == 1, total, found))
        return 0

    lax.fori_loop(0, TOK // LR, loss_rows, 0)
    packets[mv] = cols[...].T[0:8, :]

    def loss_copy(d):
        other = lax.rem(mv + d, n_vocab)
        return pltpu.make_async_remote_copy(
            src_ref=packets.at[mv],
            dst_ref=packets.at[mv],
            send_sem=lsend_sem.at[d],
            recv_sem=lrecv_sem.at[mv],
            device_id=(me, other),
            device_id_type=MESH,
        )

    for d in range(1, n_vocab):
        loss_copy(d).start()

    forward_column(1, True)
    forward_row(0)

    dcol = as_column(docs)
    key_at = lax.broadcasted_iota(jnp.int32, (TOK, TOK), 0)
    row_at = lax.broadcasted_iota(jnp.int32, (TOK, TOK), 1)
    usable = (key_at <= row_at) & (dcol[:, 0:1] == docs)
    bias[0] = jnp.where(usable, 0.0, -BIG)
    bias[1] = jnp.where(key_at == row_at, 0.0, -BIG)
    ones = jnp.ones((16, TOK), bf16)
    for s in range(STEPS):
        kd[s * TOK : (s + 1) * TOK, :] = kv_ref[s, 0]
        vd[0:HD, s * TOK : (s + 1) * TOK] = vt if s == 0 else kv_ref[s, 1].astype(f32).T.astype(bf16)
        vd[HD:VROWS, s * TOK : (s + 1) * TOK] = ones
    for copy in in_copies[3:]:
        copy.wait()

    def diag_scores(s, h, slot):
        parts = []
        for k in range(s + 1):
            sc = dg(kd[k * TOK : (k + 1) * TOK, :], qv[h, s], NT)
            sc = sc + bias[min(k, 1)]
            sb[slot, k * TOK : (k + 1) * TOK] = sc
            parts.append(jnp.max(sc.reshape(TOK // 8, 8, TOK), axis=0))
        bm[slot] = jnp.max(functools.reduce(jnp.maximum, parts), axis=0, keepdims=True)

    def diag_values(s, h, slot):
        tile = s * HEADS + h
        mx[tile] = bm[slot]
        mc = bm[slot] * C
        n = (s + 1) * TOK
        for k in range(s + 1):
            at = slice(k * TOK, (k + 1) * TOK)
            pb[slot, at] = jnp.exp2(sb[slot, at] * C - mc).astype(bf16)
        acc[tile] = dg(vd[:, 0:n], pb[slot, 0:n], NN)

    for s in range(STEPS):
        diag_scores(s, 0, 0)
        for h in range(HEADS):
            if h + 1 < HEADS:
                diag_scores(s, h + 1, (h + 1) % 2)
            diag_values(s, h, h % 2)
        if s == 1:
            forward_column(2, True)

    forward_row(1)
    arrive_core(0)
    arrive_core(1)
    groups = (jnp.minimum(me, WINDOW) + GROUP - 1) // GROUP
    first_doc = docs[:, 0:1]
    row_ok = docs == first_doc
    first_key = kv_ref[0, 0, 0:1, :]

    def prepare(g, buf, first, count):
        base = me - GROUP * (g + 1) + first
        at = [jnp.maximum(base + k, 0) for k in range(count)]
        masks = []
        for k in range(count):
            known = jnp.where(base + k >= 0, 1.0, 0.0)
            same = vall[at[k], HD:VROWS, :].astype(f32) == first_doc
            masks.append((jnp.where(same, 1.0, 0.0) * known).astype(bf16))
        mask = jnp.concatenate(masks, axis=1)
        keep = dg(mask, jnp.full((16, HD), 1.0 / 16, bf16), TN).astype(bf16)
        for k in range(count):
            gv[buf, first + k, HD:VROWS, :] = masks[k]
            gv[buf, first + k, 0:HD, :] = vall[at[k], 0:HD, :] * masks[k][0:1]
            part = keep[k * TOK : (k + 1) * TOK]
            gk[buf, first + k] = kall[at[k]] * part + first_key * (1.0 - part)

    def scores(buf, s, h, slot):
        parts = []
        for k in range(GROUP):
            at = slice(k * TOK, (k + 1) * TOK)
            sc = dg(gk[buf, k], qv[h, s], NT)
            sb[slot, at] = sc
            parts.append(jnp.max(sc.reshape(TOK // 8, 8, TOK), axis=0))
        bm[slot] = jnp.max(functools.reduce(jnp.maximum, parts), axis=0, keepdims=True)

    def step(now, after):
        buf, s, h, slot = now
        buf_after, s_after, h_after, slot_after = after
        tile = s * HEADS + h
        old = mx[tile]
        new = jnp.where(row_ok, jnp.maximum(old, bm[slot]), old)
        mx[tile] = new
        alpha = jnp.exp2((old - new) * C)
        mc = jnp.where(row_ok, new * C, BIG)
        parts = []
        for k in range(GROUP):
            at = slice(k * TOK, (k + 1) * TOK)
            sc = dg(gk[buf_after, k], qv[h_after, s_after], NT)
            sb[slot_after, at] = sc
            parts.append(jnp.max(sc.reshape(TOK // 8, 8, TOK), axis=0))
            weights = jnp.exp2(sb[slot, at] * C - mc).astype(bf16)
            part = dg(gv[buf, k], weights, NN)
            acc[tile] = acc[tile] * alpha + part if k == 0 else acc[tile] + part
        bm[slot_after] = jnp.max(functools.reduce(jnp.maximum, parts), axis=0, keepdims=True)

    prepare(0, 0, 0, GROUP)
    scores(0, 0, 0, 0)
    last = groups * STEPS - 1

    def body(t, _):
        g, s = t // STEPS, t % STEPS
        ahead = jnp.minimum(t + 1, last)
        g_next, s_next = ahead // STEPS, ahead % STEPS

        @pl.when(t == 0)
        def _():
            forward_column(3, True)

        @pl.when(t == 1)
        def _():
            forward_row(2)
            arrive_core(2, near)

        @pl.when(t == 2)
        def _():
            arrive_core(2, ~near)

        @pl.when(t == 3)
        def _():
            forward_row(3)

        @pl.when(t == 5)
        def _():
            arrive_core(3)

        prepare(jnp.minimum(g + 1, groups - 1), (g + 1) % 2, GROUP - 2 - 2 * s, 2)

        for h in range(HEADS):
            if h + 1 < HEADS:
                after = (g % 2, s, h + 1, (h + 1) % 2)
            else:
                after = (g_next % 2, s_next, 0, 0)
            step((g % 2, s, h, h % 2), after)
        return 0

    lax.fori_loop(0, groups * STEPS, body, 0)

    def finish(s, _):
        for h in range(HEADS):
            tile = s * HEADS + h
            share = 1.0 / acc[tile, HD : HD + 1, :]
            out_ref[s, :, h * HD : (h + 1) * HD] = (acc[tile, 0:HD, :] * share).T.astype(bf16)
        return 0

    lax.fori_loop(0, STEPS, finish, 0)
    for k in range(STEPS * HEADS):
        peak_ref[k // HEADS, k % HEADS : k % HEADS + 1, :] = mx[k] * SCALE

    for d in range(1, n_vocab):
        other = lax.rem(mv + n_vocab - d, n_vocab)
        pltpu.make_async_remote_copy(
            src_ref=packets.at[other],
            dst_ref=packets.at[other],
            send_sem=lsend_sem.at[d],
            recv_sem=lrecv_sem.at[other],
            device_id=(me, other),
            device_id_type=MESH,
        ).wait_recv()
    top = packets[0, 0:1, :]
    for k in range(1, n_vocab):
        top = jnp.maximum(top, packets[k, 0:1, :])
    total = jnp.zeros_like(top)
    found = jnp.zeros_like(top)
    for k in range(n_vocab):
        total = total + packets[k, 1:2, :] * jnp.exp(packets[k, 0:1, :] - top)
        found = found + packets[k, 2:3, :]
    loss_ref[...] = top + jnp.log(total) - found

    for d in range(1, n_vocab):
        loss_copy(d).wait_send()
    for slot, what in enumerate(sends):
        cond, block, target = what()

        def left(block=block, target=target, slot=slot):
            for d in descriptors(block, target, slot):
                d.wait_send()

        pl.when(cond)(left)


def local(n_vocab, queries, draft_kv, doc_ids, logits, targets):
    vocab_width = logits.shape[1]
    hbm = pl.BlockSpec(memory_space=pltpu.HBM)
    vmem = pl.BlockSpec(memory_space=pltpu.VMEM)
    out = pl.pallas_call(
        functools.partial(kernel, n_vocab, vocab_width),
        out_shape=[
            jax.ShapeDtypeStruct(queries.shape, bf16),
            jax.ShapeDtypeStruct((STEPS, HEADS, TOK), f32),
            jax.ShapeDtypeStruct((1, TOK), f32),
        ],
        in_specs=[hbm] * 5,
        out_specs=[vmem, vmem, vmem],
        scratch_shapes=[
            pltpu.VMEM((HEADS, STEPS, TOK, HD), bf16),
            pltpu.VMEM(draft_kv.shape, bf16),
            pltpu.VMEM((1, TOK), jnp.int32),
            pltpu.VMEM((1, TOK), jnp.int32),
            pltpu.VMEM(logits.shape, bf16),
            pltpu.VMEM((32, TOK, HD), bf16),
            pltpu.VMEM((32, VROWS, TOK), bf16),
            pltpu.VMEM((STEPS * TOK, HD), bf16),
            pltpu.VMEM((VROWS, STEPS * TOK), bf16),
            pltpu.VMEM((2, TOK, TOK), f32),
            pltpu.VMEM((2, GROUP, TOK, HD), bf16),
            pltpu.VMEM((2, GROUP, VROWS, TOK), bf16),
            pltpu.VMEM((2, KEYS, TOK), f32),
            pltpu.VMEM((2, KEYS, TOK), bf16),
            pltpu.VMEM((2, 1, TOK), f32),
            pltpu.VMEM((2, 1, TOK), f32),
            pltpu.VMEM((STEPS * HEADS, 1, TOK), f32),
            pltpu.VMEM((STEPS * HEADS, VROWS, TOK), f32),
            pltpu.VMEM((TOK, HD), f32),
            pltpu.VMEM((n_vocab, 8, TOK), f32),
            pltpu.SemaphoreType.DMA((3 + HEADS,)),
            pltpu.SemaphoreType.DMA((4,)),
            pltpu.SemaphoreType.DMA((32, 2)),
            pltpu.SemaphoreType.DMA((32, 2)),
            pltpu.SemaphoreType.DMA((n_vocab,)),
            pltpu.SemaphoreType.DMA((n_vocab,)),
        ],
        compiler_params=pltpu.CompilerParams(
            collective_id=0, has_side_effects=True, vmem_limit_bytes=64 * 2**20
        ),
        cost_estimate=pl.CostEstimate(
            flops=20 * 10**9, bytes_accessed=10 * 2**20, transcendentals=40 * 10**6
        ),
    )(queries, draft_kv, doc_ids.reshape(1, TOK), logits, targets.reshape(1, TOK))
    return out[0], out[1].transpose(0, 2, 1), out[2].reshape(TOK)


def solution(mesh):
    in_specs = (
        P(None, "seq", "vocab"),
        P(None, None, "seq", "vocab"),
        P("seq"),
        P("seq", "vocab"),
        P("seq"),
    )
    out_specs = (P(None, "seq", "vocab"), P(None, "seq", "vocab"), P("seq"))
    step = functools.partial(local, mesh.shape["vocab"])
    return jax.shard_map(step, mesh=mesh, in_specs=in_specs, out_specs=out_specs, check_vma=False)
```

```python
import functools

import jax
import jax.numpy as jnp
from jax import lax
from jax.experimental import pallas as pl
from jax.experimental.pallas import tpu as pltpu
from jax.sharding import PartitionSpec as P

HD = 128
STEPS = 3
TOK = 256
GROUP = 6
WIDE = 3
WINDOW = 24
KEYS = GROUP * TOK
HEADS = 8
VROWS = HD + 16
SCALE = HD ** (-0.5)
LOG2E = 1.4426950408889634
C = SCALE * LOG2E
BIG = 1e30
f32, bf16 = jnp.float32, jnp.bfloat16
NT = (((1,), (1,)), ((), ()))
NN = (((1,), (0,)), ((), ()))
TN = (((0,), (0,)), ((), ()))
MESH = pl.DeviceIdType.MESH


def dg(a, b, dims):
    return lax.dot_general(a, b, dims, preferred_element_type=f32)


def as_column(row, rows=TOK):
    wide = jnp.broadcast_to(row, (16, rows)).astype(bf16)
    return dg(wide, jnp.full((16, HD), 1.0 / 16, bf16), TN)


def kernel(
    n_vocab, vocab_width,
    q_hbm, kv_hbm, doc_hbm, lg_hbm, tg_hbm,
    out_ref, peak_ref, loss_ref,
    qv, kv_ref, doc_ref, tg_ref, lg, kall, vall, kd, vd, bias, gk, gv, sb, pb, bm, al, mx, acc, cols, packets,
    in_sem, lg_sem, send_sem, recv_sem, lsend_sem, lrecv_sem,
):
    me = lax.axis_index("seq")
    mv = lax.axis_index("vocab")
    z = me // 8
    x = (me // 2) % 4
    c = me % 2
    near = me % 8 < 2

    in_copies = [
        pltpu.make_async_copy(src, dst, in_sem.at[k])
        for k, (src, dst) in enumerate(
            ((kv_hbm, kv_ref), (doc_hbm, doc_ref), (tg_hbm, tg_ref))
        )
    ]
    in_copies += [
        pltpu.make_async_copy(
            q_hbm.at[:, :, pl.ds(h * HD, HD)], qv.at[h], in_sem.at[3 + h]
        )
        for h in range(HEADS)
    ]
    for copy in in_copies[:3]:
        copy.start()
    n_lg = 4
    lg_rows = TOK // n_lg
    lg_copies = [
        pltpu.make_async_copy(
            lg_hbm.at[pl.ds(k * lg_rows, lg_rows)], lg.at[pl.ds(k * lg_rows, lg_rows)], lg_sem.at[k]
        )
        for k in range(n_lg)
    ]
    for copy in lg_copies:
        copy.start()
    for copy in in_copies[3:]:
        copy.start()

    def dev(zz, xx, cc):
        return zz * 8 + xx * 2 + cc

    barrier = pltpu.get_barrier_semaphore()
    partners = [dev((z + d) % 4, x, c) for d in (1, 2, 3)]
    partners += [dev(z, (x + d) % 4, c) for d in (1, 2, 3)]
    partners += [dev(z, x, 1 - c)]
    for p in partners:
        pl.semaphore_signal(barrier, inc=1, device_id=(p, mv), device_id_type=MESH)
    for d in range(1, n_vocab):
        pl.semaphore_signal(
            barrier, inc=1, device_id=(me, lax.rem(mv + d, n_vocab)), device_id_type=MESH
        )

    for copy in in_copies[:3]:
        copy.wait()
    docs = doc_ref[...].astype(f32)
    kall[me] = kv_ref[0, 0]
    vt = kv_ref[0, 1].astype(f32).T.astype(bf16)
    vall[me, 0:HD, :] = vt
    vall[me, HD:VROWS, :] = jnp.broadcast_to(docs, (16, TOK)).astype(bf16)

    pl.semaphore_wait(barrier, len(partners) + n_vocab - 1)

    sends = []

    def descriptors(block, target, slot):
        return [
            pltpu.make_async_remote_copy(
                src_ref=buf.at[block],
                dst_ref=buf.at[block],
                send_sem=send_sem.at[slot, k],
                recv_sem=recv_sem.at[block, k],
                device_id=(target, mv),
                device_id_type=MESH,
            )
            for k, buf in enumerate((kall, vall))
        ]

    def send(what):
        slot = len(sends)
        sends.append(what)
        cond, block, target = what()

        def go():
            for d in descriptors(block, target, slot):
                d.start()

        pl.when(cond)(go)

    def arrived(cond, block):
        def go():
            for d in descriptors(block, me, 0):
                d.wait_recv()

        pl.when(cond)(go)

    def wanted(dz, xx, at_x):
        if dz == 0:
            return xx < at_x
        if dz == 3:
            return (z >= 3) & (xx >= at_x)
        return z >= dz

    def plane_send(dz):
        return z + dz <= 3, me, dev(z + dz, x, c)

    def column_send(dz, d):
        xx = (x + d) % 4
        return wanted(dz, x, xx), dev(z - dz, x, c), dev(z, xx, c)

    def core_send(dz, d):
        xx = (x + d) % 4
        if d:
            cond = wanted(dz, xx, x)
        else:
            cond = z >= dz if dz else c == 0
        return cond, dev(z - dz, xx, c), dev(z, x, 1 - c)

    def forward_column(dz, arrive):
        if arrive:
            arrived(z >= dz, dev(z - dz, x, c))
        for d in (1, 3, 2):
            send(functools.partial(column_send, dz, d))
        send(functools.partial(core_send, dz, 0))

    def forward_row(dz):
        for d in (1, 3, 2):
            xx = (x + d) % 4
            block = dev(z - dz, xx, c)
            arrived(wanted(dz, xx, x), block)
            send(functools.partial(core_send, dz, d))

    def arrive_core(dz, these=None):
        for d in (0, 1, 3, 2):
            xx = (x + d) % 4
            if d:
                cond = wanted(dz, xx, x)
            else:
                cond = z >= dz if dz else c == 1
            arrived(cond if these is None else cond & these, dev(z - dz, xx, 1 - c))

    for dz in (1, 2, 3):
        send(functools.partial(plane_send, dz))
    forward_column(0, False)

    target = tg_ref[...] - mv * vocab_width
    inside = (target >= 0) & (target < vocab_width)
    target = jnp.where(inside, target, 0)
    hi = target // 256
    lo = target - hi * 256
    tcol = as_column(hi.astype(f32)) * 256.0 + as_column(lo.astype(f32))
    tcol = jnp.where(as_column(inside.astype(f32)) > 0.5, tcol, -1.0)
    cols[...] = tcol
    LR, LC = 64, 128
    for copy in lg_copies:
        copy.wait()

    def loss_rows(k, _):
        rows = pl.ds(pl.multiple_of(k * LR, LR), LR)
        top = lg[rows, 0:LC]
        for ch in range(1, vocab_width // LC):
            top = jnp.maximum(top, lg[rows, ch * LC : (ch + 1) * LC])
        top = jnp.max(top.astype(f32), axis=1, keepdims=True)
        want = cols[rows, 0:1].astype(jnp.int32)
        lane = lax.broadcasted_iota(jnp.int32, (LR, LC), 1)
        total = jnp.zeros((LR, LC), f32)
        found = jnp.zeros((LR, LC), f32)
        for ch in range(vocab_width // LC):
            v = lg[rows, ch * LC : (ch + 1) * LC].astype(f32)
            total = total + jnp.exp(v - top)
            found = found + jnp.where(lane == want - ch * LC, v, 0.0)
        total = jnp.sum(total, axis=1, keepdims=True)
        found = jnp.sum(found, axis=1, keepdims=True)
        at = lax.broadcasted_iota(jnp.int32, (LR, HD), 1)
        cols[rows, :] = jnp.where(at == 0, top, jnp.where(at == 1, total, found))
        return 0

    lax.fori_loop(0, TOK // LR, loss_rows, 0)
    packets[mv] = cols[...].T[0:8, :]

    def loss_copy(d):
        other = lax.rem(mv + d, n_vocab)
        return pltpu.make_async_remote_copy(
            src_ref=packets.at[mv],
            dst_ref=packets.at[mv],
            send_sem=lsend_sem.at[d],
            recv_sem=lrecv_sem.at[mv],
            device_id=(me, other),
            device_id_type=MESH,
        )

    for d in range(1, n_vocab):
        loss_copy(d).start()

    forward_column(1, True)
    forward_row(0)

    dcol = as_column(docs)
    key_at = lax.broadcasted_iota(jnp.int32, (TOK, TOK), 0)
    row_at = lax.broadcasted_iota(jnp.int32, (TOK, TOK), 1)
    usable = (key_at <= row_at) & (dcol[:, 0:1] == docs)
    bias[0] = jnp.where(usable, 0.0, -BIG)
    bias[1] = jnp.where(key_at == row_at, 0.0, -BIG)
    ones = jnp.ones((16, TOK), bf16)
    for s in range(STEPS):
        kd[s * TOK : (s + 1) * TOK, :] = kv_ref[s, 0]
        vd[0:HD, s * TOK : (s + 1) * TOK] = vt if s == 0 else kv_ref[s, 1].astype(f32).T.astype(bf16)
        vd[HD:VROWS, s * TOK : (s + 1) * TOK] = ones
    for copy in in_copies[3:]:
        copy.wait()

    def diag_scores(s, h, slot):
        parts = []
        for k in range(s + 1):
            sc = dg(kd[k * TOK : (k + 1) * TOK, :], qv[h, s], NT)
            sc = sc + bias[min(k, 1)]
            sb[slot, k * TOK : (k + 1) * TOK] = sc
            parts.append(jnp.max(sc.reshape(TOK // 8, 8, TOK), axis=0))
        bm[slot] = jnp.max(functools.reduce(jnp.maximum, parts), axis=0, keepdims=True)

    def diag_values(s, h, slot):
        tile = s * HEADS + h
        mx[tile] = bm[slot]
        mc = bm[slot] * C
        n = (s + 1) * TOK
        for k in range(s + 1):
            at = slice(k * TOK, (k + 1) * TOK)
            pb[slot, at] = jnp.exp2(sb[slot, at] * C - mc).astype(bf16)
        acc[tile] = dg(vd[:, 0:n], pb[slot, 0:n], NN)

    for s in range(STEPS):
        diag_scores(s, 0, 0)
        for h in range(HEADS):
            if h + 1 < HEADS:
                diag_scores(s, h + 1, (h + 1) % 2)
            diag_values(s, h, h % 2)
        if s == 1:
            forward_column(2, True)

    forward_row(1)
    arrive_core(0)
    arrive_core(1)
    groups = (jnp.minimum(me, WINDOW) + GROUP - 1) // GROUP
    first_doc = docs[:, 0:1]
    row_ok = docs == first_doc
    first_key = kv_ref[0, 0, 0:1, :]

    def prepare(g, buf, first, count):
        base = me - GROUP * (g + 1) + first
        at = [jnp.maximum(base + k, 0) for k in range(count)]
        masks = []
        for k in range(count):
            known = jnp.where(base + k >= 0, 1.0, 0.0)
            same = vall[at[k], HD:VROWS, :].astype(f32) == first_doc
            masks.append((jnp.where(same, 1.0, 0.0) * known).astype(bf16))
        mask = jnp.concatenate(masks, axis=1)
        keep = dg(mask, jnp.full((16, HD), 1.0 / 16, bf16), TN).astype(bf16)
        for k in range(count):
            gv[buf, first + k, HD:VROWS, :] = masks[k]
            gv[buf, first + k, 0:HD, :] = vall[at[k], 0:HD, :] * masks[k][0:1]
            part = keep[k * TOK : (k + 1) * TOK]
            gk[buf, first + k] = kall[at[k]] * part + first_key * (1.0 - part)

    def scores(buf, s, h, slot):
        parts = []
        for k in range(GROUP):
            at = slice(k * TOK, (k + 1) * TOK)
            sc = dg(gk[buf, k], qv[h, s], NT)
            sb[slot, at] = sc
            parts.append(jnp.max(sc.reshape(TOK // 8, 8, TOK), axis=0))
        bm[slot] = jnp.max(functools.reduce(jnp.maximum, parts), axis=0, keepdims=True)

    def step(now, after):
        buf, s, h, slot = now
        buf_after, s_after, h_after, slot_after = after
        tile = s * HEADS + h
        old = mx[tile]
        new = jnp.where(row_ok, jnp.maximum(old, bm[slot]), old)
        mx[tile] = new
        alpha = jnp.exp2((old - new) * C)
        mc = jnp.where(row_ok, new * C, BIG)
        parts = []
        for k in range(0, GROUP, WIDE):
            at = slice(k * TOK, (k + WIDE) * TOK)
            keys = gk[buf_after, k : k + WIDE].reshape(WIDE * TOK, HD)
            sc = dg(keys, qv[h_after, s_after], NT)
            sb[slot_after, at] = sc
            parts.append(jnp.max(sc.reshape(WIDE * TOK // 8, 8, TOK), axis=0))
            weights = jnp.exp2(sb[slot, at] * C - mc).astype(bf16)
            part = dg(gv[buf, k], weights[:TOK], NN)
            for b in range(1, WIDE):
                part = part + dg(gv[buf, k + b], weights[b * TOK : (b + 1) * TOK], NN)
            acc[tile] = acc[tile] * alpha + part if k == 0 else acc[tile] + part
        bm[slot_after] = jnp.max(functools.reduce(jnp.maximum, parts), axis=0, keepdims=True)

    prepare(0, 0, 0, GROUP)
    scores(0, 0, 0, 0)
    last = groups * STEPS - 1

    def body(t, _):
        g, s = t // STEPS, t % STEPS
        ahead = jnp.minimum(t + 1, last)
        g_next, s_next = ahead // STEPS, ahead % STEPS

        @pl.when(t == 0)
        def _():
            forward_column(3, True)

        @pl.when(t == 1)
        def _():
            forward_row(2)
            arrive_core(2, near)

        @pl.when(t == 2)
        def _():
            arrive_core(2, ~near)

        @pl.when(t == 3)
        def _():
            forward_row(3)

        @pl.when(t == 5)
        def _():
            arrive_core(3)

        prepare(jnp.minimum(g + 1, groups - 1), (g + 1) % 2, GROUP - 2 - 2 * s, 2)

        for h in range(HEADS):
            if h + 1 < HEADS:
                after = (g % 2, s, h + 1, (h + 1) % 2)
            else:
                after = (g_next % 2, s_next, 0, 0)
            step((g % 2, s, h, h % 2), after)
        return 0

    lax.fori_loop(0, groups * STEPS, body, 0)

    def finish(s, _):
        for h in range(HEADS):
            tile = s * HEADS + h
            share = 1.0 / acc[tile, HD : HD + 1, :]
            out_ref[s, :, h * HD : (h + 1) * HD] = (acc[tile, 0:HD, :] * share).T.astype(bf16)
        return 0

    lax.fori_loop(0, STEPS, finish, 0)
    for k in range(STEPS * HEADS):
        peak_ref[k // HEADS, k % HEADS : k % HEADS + 1, :] = mx[k] * SCALE

    for d in range(1, n_vocab):
        other = lax.rem(mv + n_vocab - d, n_vocab)
        pltpu.make_async_remote_copy(
            src_ref=packets.at[other],
            dst_ref=packets.at[other],
            send_sem=lsend_sem.at[d],
            recv_sem=lrecv_sem.at[other],
            device_id=(me, other),
            device_id_type=MESH,
        ).wait_recv()
    top = packets[0, 0:1, :]
    for k in range(1, n_vocab):
        top = jnp.maximum(top, packets[k, 0:1, :])
    total = jnp.zeros_like(top)
    found = jnp.zeros_like(top)
    for k in range(n_vocab):
        total = total + packets[k, 1:2, :] * jnp.exp(packets[k, 0:1, :] - top)
        found = found + packets[k, 2:3, :]
    loss_ref[...] = top + jnp.log(total) - found

    for d in range(1, n_vocab):
        loss_copy(d).wait_send()
    for slot, what in enumerate(sends):
        cond, block, target = what()

        def left(block=block, target=target, slot=slot):
            for d in descriptors(block, target, slot):
                d.wait_send()

        pl.when(cond)(left)


def local(n_vocab, queries, draft_kv, doc_ids, logits, targets):
    vocab_width = logits.shape[1]
    hbm = pl.BlockSpec(memory_space=pltpu.HBM)
    vmem = pl.BlockSpec(memory_space=pltpu.VMEM)
    out = pl.pallas_call(
        functools.partial(kernel, n_vocab, vocab_width),
        out_shape=[
            jax.ShapeDtypeStruct(queries.shape, bf16),
            jax.ShapeDtypeStruct((STEPS, HEADS, TOK), f32),
            jax.ShapeDtypeStruct((1, TOK), f32),
        ],
        in_specs=[hbm] * 5,
        out_specs=[vmem, vmem, vmem],
        scratch_shapes=[
            pltpu.VMEM((HEADS, STEPS, TOK, HD), bf16),
            pltpu.VMEM(draft_kv.shape, bf16),
            pltpu.VMEM((1, TOK), jnp.int32),
            pltpu.VMEM((1, TOK), jnp.int32),
            pltpu.VMEM(logits.shape, bf16),
            pltpu.VMEM((32, TOK, HD), bf16),
            pltpu.VMEM((32, VROWS, TOK), bf16),
            pltpu.VMEM((STEPS * TOK, HD), bf16),
            pltpu.VMEM((VROWS, STEPS * TOK), bf16),
            pltpu.VMEM((2, TOK, TOK), f32),
            pltpu.VMEM((2, GROUP, TOK, HD), bf16),
            pltpu.VMEM((2, GROUP, VROWS, TOK), bf16),
            pltpu.VMEM((2, KEYS, TOK), f32),
            pltpu.VMEM((2, KEYS, TOK), bf16),
            pltpu.VMEM((2, 1, TOK), f32),
            pltpu.VMEM((2, 1, TOK), f32),
            pltpu.VMEM((STEPS * HEADS, 1, TOK), f32),
            pltpu.VMEM((STEPS * HEADS, VROWS, TOK), f32),
            pltpu.VMEM((TOK, HD), f32),
            pltpu.VMEM((n_vocab, 8, TOK), f32),
            pltpu.SemaphoreType.DMA((3 + HEADS,)),
            pltpu.SemaphoreType.DMA((4,)),
            pltpu.SemaphoreType.DMA((32, 2)),
            pltpu.SemaphoreType.DMA((32, 2)),
            pltpu.SemaphoreType.DMA((n_vocab,)),
            pltpu.SemaphoreType.DMA((n_vocab,)),
        ],
        compiler_params=pltpu.CompilerParams(
            collective_id=0, has_side_effects=True, vmem_limit_bytes=64 * 2**20
        ),
        cost_estimate=pl.CostEstimate(
            flops=20 * 10**9, bytes_accessed=10 * 2**20, transcendentals=40 * 10**6
        ),
    )(queries, draft_kv, doc_ids.reshape(1, TOK), logits, targets.reshape(1, TOK))
    return out[0], out[1].transpose(0, 2, 1), out[2].reshape(TOK)


def solution(mesh):
    in_specs = (
        P(None, "seq", "vocab"),
        P(None, None, "seq", "vocab"),
        P("seq"),
        P("seq", "vocab"),
        P("seq"),
    )
    out_specs = (P(None, "seq", "vocab"), P(None, "seq", "vocab"), P("seq"))
    step = functools.partial(local, mesh.shape["vocab"])
    return jax.shard_map(step, mesh=mesh, in_specs=in_specs, out_specs=out_specs, check_vma=False)
```
